32 devices in a mesh: seq: 8 (over y, x, core), ch: 4 (over z).
Axes of the slice: x: 2, y: 2, z: 4, core: 2. Of those that a mesh axis runs over, the one named last changes fastest.
Arguments:
- tokens: bfloat16 [3072, 8192], P('seq', 'ch'), may hold values from -6 to 6
- in_weight: bfloat16 [3, 8192, 1024], P(None, 'seq', 'ch'), may hold values from -0.0625 to 0.0625
- short_filter: float32 [7, 3, 1024], P(None, None, 'ch'), may hold values from -2.4 to 2.4
- long_taps: float32 [128, 1024], P(None, 'ch'), may hold values from -0.5 to 0.5
- decay_rate: float32 [16, 1024], P(None, 'ch'), may hold values from 6.510417e-06 to 0.033333335
- residue: float32 [16, 1024], P(None, 'ch'), may hold values from -1.5 to 1.5
Outputs:
- gated: bfloat16 [3072, 1024], P('seq', 'ch')
The draws below stay inside these ranges and needn't reach their ends.
All inputs are finite; a program needn't handle non-finite values.
Results may differ from the reference program's by a relative error of at most 0.017.
Values may be sent and summed in bfloat16 or wider, within the bound.
A program may use at most 64 MiB of HBM per device.

```python
import math
import jax
import jax.numpy as jnp
from jax import lax

D = 8192
MODES = 16
TAPS = 128
SHORT = 7
DW = 1024
TOKENS = 3072


def level_of(stream_key, extent, cuts, smallest, largest):
    loudness = 1.0
    for dim, parts in cuts:
        heights = jax.random.uniform(jax.random.fold_in(jax.random.fold_in(stream_key, 6), dim), (parts,), jnp.float32, smallest / len(cuts), largest / len(cuts))
        loudness = loudness * jnp.repeat(jnp.exp(heights), extent[dim] // parts).reshape((-1,) + (1,) * (len(extent) - 1 - dim))
    return loudness


def scatter_about(key, dims, scale, limit, cuts=(), held_as=jnp.bfloat16):
    drawn = jax.random.normal(key, dims, jnp.float32) * scale
    if len(cuts) > 0:
        drawn = level_of(key, dims, cuts, -0.22, 0.18) * drawn
    return jnp.clip(drawn, min=-limit, max=limit).astype(held_as)


def setup_inputs(seed: int = 0) -> dict:
    key_list = jax.random.split(jax.random.key(seed), 7)
    return {
        "tokens": scatter_about(key_list[0], (TOKENS, D), 1.0, 6.0, ((0, 8), (1, 4))),
        "in_weight": scatter_about(key_list[1], (3, D, DW), D ** -0.5, 0.0625, ((1, 8), (2, 4))),
        "short_filter": scatter_about(key_list[2], (SHORT, 3, DW), 0.4, 2.4, ((2, 4),), jnp.float32),
        "long_taps": scatter_about(key_list[3], (TAPS, DW), TAPS ** -0.5, 0.5, ((1, 4),), jnp.float32),
        "decay_rate": jnp.clip(jnp.exp(math.log(0.033333335) - 8.54091 * jax.random.uniform(key_list[4], (MODES, DW), jnp.float32) ** level_of(key_list[4], (MODES, DW), ((1, 4),), -0.2, 0.2)), 6.510416824312415e-06, 0.033333335),
        "residue": scatter_about(key_list[5], (MODES, DW), MODES ** -0.5, 1.5, ((1, 4),), jnp.float32),
    }


def causal_taps(signal, kernel):
    length = signal.shape[0]
    width = kernel.shape[0]
    padded = jnp.concatenate([jnp.zeros((width - 1, signal.shape[1]), signal.dtype), signal], axis=0)

    def add_tap(index, running):
        window = lax.dynamic_slice_in_dim(padded, (width - 1 - index).astype(jnp.int32), length, 0)
        weights = lax.dynamic_slice_in_dim(kernel, index.astype(jnp.int32), 1, 0)
        return running + weights * window
    return lax.fori_loop(jnp.int32(0), jnp.int32(width), add_tap, jnp.zeros(signal.shape, signal.dtype))

def reference(tokens, in_weight, short_filter, long_taps, decay_rate, residue):
    blocks = [jnp.dot(tokens, in_weight[which], preferred_element_type=jnp.float32) for which in range(3)]
    features = jnp.concatenate(blocks, axis=1).astype(jnp.bfloat16)
    short_taps = short_filter.reshape(SHORT, 3 * DW)
    filtered = causal_taps(features.astype(jnp.float32), short_taps)
    product = (filtered[:, DW:2 * DW] * filtered[:, 2 * DW:]).astype(jnp.bfloat16)
    product_f = product.astype(jnp.float32)
    explicit = causal_taps(product_f, long_taps)
    coef = residue * jnp.sqrt(-jnp.expm1(-2.0 * decay_rate))
    lam = jnp.exp(-decay_rate)
    mode_index = jnp.arange(MODES).astype(jnp.float32)
    omega = math.pi * (2.0 * mode_index + 1.0) / (2.0 * MODES)
    turn_cos = jnp.cos(omega)[:, None]
    turn_sin = jnp.sin(omega)[:, None]

    def advance(state, row):
        real_part, imag_part = state
        new_real = lam * (turn_cos * real_part - turn_sin * imag_part) + row[None, :]
        new_imag = lam * (turn_sin * real_part + turn_cos * imag_part)
        return ((new_real, new_imag), lax.optimization_barrier(jnp.sum(coef * new_real, axis=0)))
    start_state = (jnp.zeros((MODES, DW), jnp.float32), jnp.zeros((MODES, DW), jnp.float32))
    final_state, modal = lax.scan(advance, start_state, product_f)
    return (filtered[:, :DW] * (explicit + modal)).astype(jnp.bfloat16)
```

```python
import math

import jax
import jax.numpy as jnp
import numpy as np
from jax import lax
from jax.sharding import PartitionSpec as P

TAPS = 128
SHORT = 7


def from_behind(value, axis):
    count = lax.axis_size(axis)
    return lax.ppermute(value, axis, [(source, source + 1) for source in range(count - 1)])


def flip(value, mask):
    count = lax.axis_size("seq")
    return lax.ppermute(value, "seq", [(s, s ^ mask) for s in range(count)])


def gather_weights(weight):
    count = lax.axis_size("seq")
    if count != 8:
        return lax.all_gather(weight, "seq", axis=1, tiled=True)
    me = lax.axis_index("seq")
    over_x = flip(weight, 2)
    over_y = flip(weight, 4)
    onward = jnp.where(me % 2 == 0, over_x, over_y)
    diagonal = lax.ppermute(onward, "seq", [(s, s ^ (4 if s % 2 == 0 else 2)) for s in range(8)])
    pieces = [(0, weight), (2, over_x), (4, over_y), (6, diagonal)]
    pieces += [(mask ^ 1, flip(piece, 1)) for mask, piece in pieces]
    depth = weight.shape[1]
    whole = jnp.zeros((3, count * depth, weight.shape[2]), weight.dtype)
    for mask, piece in pieces:
        whole = lax.dynamic_update_slice(whole, piece, (0, (me ^ mask) * depth, 0))
    return whole


def phase_angle(steps, mode_count):
    period = 4 * mode_count
    odd_numbers = 2 * jnp.arange(mode_count) + 1
    turns = steps[:, None] % period * odd_numbers[None, :] % period
    return turns.astype(jnp.float32) * (math.pi / (2 * mode_count))


def damped(decay_rate, steps):
    angle = phase_angle(steps, decay_rate.shape[0])
    magnitude = jnp.exp(-decay_rate[None] * steps.astype(jnp.float32)[:, None, None])
    return (magnitude * jnp.cos(angle)[:, :, None], magnitude * jnp.sin(angle)[:, :, None])


def fourier(rows, initial, count):
    turns = np.outer(2 * np.arange(rows) + 1, np.arange(initial, initial + count)) % (4 * rows)
    angle = turns * (math.pi / (2 * rows))
    return np.cos(angle).astype(np.float32), np.sin(angle).astype(np.float32)


def times(matrix, value):
    return jnp.dot(
        jnp.asarray(matrix), value, precision=lax.Precision.HIGH, preferred_element_type=jnp.float32
    )


def on_device(tokens, in_weight, short_filter, long_taps, decay_rate, residue):
    place = lax.axis_index("seq")
    count = lax.axis_size("seq")
    rows = tokens.shape[0]
    width = in_weight.shape[2]
    modes = decay_rate.shape[0]
    half = 2 * modes
    laps = rows // half

    gathered = lax.all_gather(tokens, "ch", axis=1, tiled=True)
    weights = gather_weights(in_weight)

    coef = residue * jnp.sqrt(-jnp.expm1(-2.0 * decay_rate))
    near_cos, near_sin = damped(decay_rate, jnp.arange(half + 1))
    sign = jnp.where(jnp.arange(laps) % 2 == 0, 1.0, -1.0)[:, None, None]
    far = sign * jnp.exp(
        -decay_rate[None] * (half * jnp.arange(laps)).astype(jnp.float32)[:, None, None]
    )
    near_kernel = jnp.sum(near_cos[:half, None] * far[None] * coef[None, None], axis=2)
    modal_kernel = near_kernel.transpose(1, 0, 2).reshape(rows, width)
    kernel = modal_kernel.at[:TAPS].add(long_taps)
    cos, sin = fourier(rows, 0, rows)
    cos_sin = np.concatenate([cos, -sin], axis=0)
    spectrum = times(cos_sin, kernel) * (1.0 / rows)
    taps_spectrum = times(cos_sin[:, :TAPS], long_taps) * (1.0 / rows)
    kernel_re, kernel_im = spectrum[:rows], spectrum[rows:]
    taps_re, taps_im = taps_spectrum[:rows], taps_spectrum[rows:]
    behind = place - 1 - jnp.arange(count)
    since_re, since_im = damped(decay_rate, jnp.maximum(behind, 0) * rows)
    before = (behind >= 0)[:, None, None]
    since_re = jnp.where(before, since_re, 0.0)
    since_im = jnp.where(before, since_im, 0.0)
    ahead_re = (coef[None] * near_cos[1:]).transpose(1, 0, 2)
    ahead_im = (coef[None] * near_sin[1:]).transpose(1, 0, 2)
    back_re, back_im, back_far = near_cos[:half][::-1], near_sin[:half][::-1], far[::-1]

    blocks = [jnp.dot(gathered, weights[j], preferred_element_type=jnp.float32) for j in range(3)]
    features = jnp.concatenate(blocks, axis=1).astype(jnp.bfloat16)
    head = from_behind(features[rows - (SHORT - 1) :], "seq")
    extended = jnp.concatenate([head, features], axis=0).astype(jnp.float32)
    short_taps = short_filter.reshape(SHORT, 3 * width)
    filtered = sum(
        short_taps[i][None] * extended[SHORT - 1 - i : SHORT - 1 - i + rows] for i in range(SHORT)
    )
    product = (filtered[:, width : 2 * width] * filtered[:, 2 * width :]).astype(jnp.bfloat16)

    tail = from_behind(product[rows - TAPS :], "seq").astype(jnp.float32)
    product_f = product.astype(jnp.float32)
    by_lap = product_f.reshape(laps, half, width)
    folded = jnp.sum(back_far[:, None] * by_lap[:, :, None, :], axis=0)
    own = jnp.concatenate(
        [jnp.sum(back_re * folded, axis=0), jnp.sum(back_im * folded, axis=0)], axis=0
    ).astype(jnp.bfloat16)
    states = lax.all_gather(own, "seq").astype(jnp.float32)

    seen = times(cos_sin, product_f)
    seen_re, seen_im = seen[:rows], seen[rows:]
    tail_cos, tail_sin = fourier(rows, -TAPS, TAPS)
    halo = times(np.concatenate([tail_cos, -tail_sin], axis=0), tail)
    halo_re, halo_im = halo[:rows], halo[rows:]
    out_re = kernel_re * seen_re - kernel_im * seen_im + taps_re * halo_re - taps_im * halo_im
    out_im = kernel_re * seen_im + kernel_im * seen_re + taps_re * halo_im + taps_im * halo_re
    local = times(
        np.concatenate([cos.T, -sin.T], axis=1), jnp.concatenate([out_re, out_im], axis=0)
    )

    state_re, state_im = states[:, :modes], states[:, modes:]
    inflow_re = jnp.sum(since_re * state_re - since_im * state_im, axis=0)
    inflow_im = jnp.sum(since_re * state_im + since_im * state_re, axis=0)
    ahead = ahead_re * inflow_re[:, None] - ahead_im * inflow_im[:, None]
    inflow = jnp.sum(far[:, :, None, :] * ahead[None], axis=1).reshape(rows, width)
    return (filtered[:, :width] * (local + inflow)).astype(jnp.bfloat16)


def solution(mesh):
    placed = (
        P("seq", "ch"),
        P(None, "seq", "ch"),
        P(None, None, "ch"),
        P(None, "ch"),
        P(None, "ch"),
        P(None, "ch"),
    )
    return jax.shard_map(
        on_device, mesh=mesh, in_specs=placed, out_specs=P("seq", "ch"), check_vma=False
    )
```

```python
import math

import jax
import jax.numpy as jnp
import numpy as np
from jax import lax
from jax.sharding import PartitionSpec as P

TAPS = 128
SHORT = 7


def from_behind(value, axis):
    count = lax.axis_size(axis)
    return lax.ppermute(value, axis, [(source, source + 1) for source in range(count - 1)])


def flip(value, mask):
    count = lax.axis_size("seq")
    return lax.ppermute(value, "seq", [(s, s ^ mask) for s in range(count)])


def gather_weights(weight):
    count = lax.axis_size("seq")
    if count != 8:
        return lax.all_gather(weight, "seq", axis=1, tiled=True)
    me = lax.axis_index("seq")
    over_x = flip(weight, 2)
    over_y = flip(weight, 4)
    onward = jnp.where(me % 2 == 0, over_x, over_y)
    diagonal = lax.ppermute(onward, "seq", [(s, s ^ (4 if s % 2 == 0 else 2)) for s in range(8)])
    pieces = [(0, weight), (2, over_x), (4, over_y), (6, diagonal)]
    pieces += [(mask ^ 1, flip(piece, 1)) for mask, piece in pieces]
    depth = weight.shape[1]
    whole = jnp.zeros((3, count * depth, weight.shape[2]), weight.dtype)
    for mask, piece in pieces:
        whole = lax.dynamic_update_slice(whole, piece, (0, (me ^ mask) * depth, 0))
    return whole


def project(tokens, in_weight):
    count = lax.axis_size("ch")
    if count != 4:
        gathered = lax.all_gather(tokens, "ch", axis=1, tiled=True)
        weights = gather_weights(in_weight)
        blocks = [
            jnp.dot(gathered, weights[j], preferred_element_type=jnp.float32) for j in range(3)
        ]
        return jnp.concatenate(blocks, axis=1)
    me = lax.axis_index("ch")
    depth = tokens.shape[1]

    def shift(value, pairs):
        return lax.ppermute(value, "ch", pairs)

    up_1 = shift(tokens, [(0, 1), (1, 2), (2, 3)])
    down_1 = shift(tokens, [(1, 0), (2, 1), (3, 2)])
    up_2 = shift(up_1, [(1, 2), (2, 3)])
    down_2 = shift(down_1, [(1, 0), (2, 1)])
    up_3 = shift(up_2, [(2, 3)])
    down_3 = shift(down_2, [(1, 0)])
    weights = gather_weights(in_weight)

    def add_rows(value, source):
        portion = lax.dynamic_slice_in_dim(weights, source * depth, depth, 1)
        return jnp.concatenate(
            [jnp.dot(value, portion[j], preferred_element_type=jnp.float32) for j in range(3)],
            axis=1,
        )

    total = add_rows(tokens, me)
    total += add_rows(up_1, (me + 3) % 4) + add_rows(down_1, (me + 1) % 4)
    total += add_rows(up_2 + down_2, (me + 2) % 4)
    return total + add_rows(up_3 + down_3, 3 - me)


def phase_angle(steps, mode_count):
    period = 4 * mode_count
    odd_numbers = 2 * jnp.arange(mode_count) + 1
    turns = steps[:, None] % period * odd_numbers[None, :] % period
    return turns.astype(jnp.float32) * (math.pi / (2 * mode_count))


def damped(decay_rate, steps):
    angle = phase_angle(steps, decay_rate.shape[0])
    magnitude = jnp.exp(-decay_rate[None] * steps.astype(jnp.float32)[:, None, None])
    return (magnitude * jnp.cos(angle)[:, :, None], magnitude * jnp.sin(angle)[:, :, None])


def fourier(rows, initial, count):
    turns = np.outer(2 * np.arange(rows) + 1, np.arange(initial, initial + count)) % (4 * rows)
    angle = turns * (math.pi / (2 * rows))
    return np.cos(angle).astype(np.float32), np.sin(angle).astype(np.float32)


def times(matrix, value):
    return jnp.dot(
        jnp.asarray(matrix), value, precision=lax.Precision.HIGH, preferred_element_type=jnp.float32
    )


def on_device(tokens, in_weight, short_filter, long_taps, decay_rate, residue):
    place = lax.axis_index("seq")
    count = lax.axis_size("seq")
    rows = tokens.shape[0]
    width = in_weight.shape[2]
    modes = decay_rate.shape[0]
    half = 2 * modes
    laps = rows // half

    features = project(tokens, in_weight).astype(jnp.bfloat16)

    coef = residue * jnp.sqrt(-jnp.expm1(-2.0 * decay_rate))
    near_cos, near_sin = damped(decay_rate, jnp.arange(half + 1))
    sign = jnp.where(jnp.arange(laps) % 2 == 0, 1.0, -1.0)[:, None, None]
    far = sign * jnp.exp(
        -decay_rate[None] * (half * jnp.arange(laps)).astype(jnp.float32)[:, None, None]
    )
    near_kernel = jnp.sum(near_cos[:half, None] * far[None] * coef[None, None], axis=2)
    modal_kernel = near_kernel.transpose(1, 0, 2).reshape(rows, width)
    kernel = modal_kernel.at[:TAPS].add(long_taps)
    cos, sin = fourier(rows, 0, rows)
    cos_sin = np.concatenate([cos, -sin], axis=0)
    spectrum = times(cos_sin, kernel) * (1.0 / rows)
    taps_spectrum = times(cos_sin[:, :TAPS], long_taps) * (1.0 / rows)
    kernel_re, kernel_im = spectrum[:rows], spectrum[rows:]
    taps_re, taps_im = taps_spectrum[:rows], taps_spectrum[rows:]
    behind = place - 1 - jnp.arange(count)
    since_re, since_im = damped(decay_rate, jnp.maximum(behind, 0) * rows)
    before = (behind >= 0)[:, None, None]
    since_re = jnp.where(before, since_re, 0.0)
    since_im = jnp.where(before, since_im, 0.0)
    ahead_re = (coef[None] * near_cos[1:]).transpose(1, 0, 2)
    ahead_im = (coef[None] * near_sin[1:]).transpose(1, 0, 2)
    back_re, back_im, back_far = near_cos[:half][::-1], near_sin[:half][::-1], far[::-1]

    head = from_behind(features[rows - (SHORT - 1) :], "seq")
    extended = jnp.concatenate([head, features], axis=0).astype(jnp.float32)
    short_taps = short_filter.reshape(SHORT, 3 * width)
    filtered = sum(
        short_taps[i][None] * extended[SHORT - 1 - i : SHORT - 1 - i + rows] for i in range(SHORT)
    )
    product = (filtered[:, width : 2 * width] * filtered[:, 2 * width :]).astype(jnp.bfloat16)

    tail = from_behind(product[rows - TAPS :], "seq").astype(jnp.float32)
    product_f = product.astype(jnp.float32)
    by_lap = product_f.reshape(laps, half, width)
    folded = jnp.sum(back_far[:, None] * by_lap[:, :, None, :], axis=0)
    own = jnp.concatenate(
        [jnp.sum(back_re * folded, axis=0), jnp.sum(back_im * folded, axis=0)], axis=0
    ).astype(jnp.bfloat16)
    states = lax.all_gather(own, "seq").astype(jnp.float32)

    seen = times(cos_sin, product_f)
    seen_re, seen_im = seen[:rows], seen[rows:]
    tail_cos, tail_sin = fourier(rows, -TAPS, TAPS)
    halo = times(np.concatenate([tail_cos, -tail_sin], axis=0), tail)
    halo_re, halo_im = halo[:rows], halo[rows:]
    out_re = kernel_re * seen_re - kernel_im * seen_im + taps_re * halo_re - taps_im * halo_im
    out_im = kernel_re * seen_im + kernel_im * seen_re + taps_re * halo_im + taps_im * halo_re
    local = times(
        np.concatenate([cos.T, -sin.T], axis=1), jnp.concatenate([out_re, out_im], axis=0)
    )

    state_re, state_im = states[:, :modes], states[:, modes:]
    inflow_re = jnp.sum(since_re * state_re - since_im * state_im, axis=0)
    inflow_im = jnp.sum(since_re * state_im + since_im * state_re, axis=0)
    ahead = ahead_re * inflow_re[:, None] - ahead_im * inflow_im[:, None]
    inflow = jnp.sum(far[:, :, None, :] * ahead[None], axis=1).reshape(rows, width)
    return (filtered[:, :width] * (local + inflow)).astype(jnp.bfloat16)


def solution(mesh):
    placed = (
        P("seq", "ch"),
        P(None, "seq", "ch"),
        P(None, None, "ch"),
        P(None, "ch"),
        P(None, "ch"),
        P(None, "ch"),
    )
    return jax.shard_map(
        on_device, mesh=mesh, in_specs=placed, out_specs=P("seq", "ch"), check_vma=False
    )
```

```python
import math

import jax
import jax.numpy as jnp
import numpy as np
from jax import lax
from jax.experimental import pallas as pl
from jax.experimental.pallas import tpu as pltpu
from jax.sharding import PartitionSpec as P

TAPS = 128
SHORT = 7


def from_behind(value, axis):
    count = lax.axis_size(axis)
    return lax.ppermute(value, axis, [(source, source + 1) for source in range(count - 1)])


def flip(value, mask):
    count = lax.axis_size("seq")
    return lax.ppermute(value, "seq", [(s, s ^ mask) for s in range(count)])


def gather_weights(weight):
    count = lax.axis_size("seq")
    if count != 8:
        return lax.all_gather(weight, "seq", axis=1, tiled=True)
    me = lax.axis_index("seq")
    over_x = flip(weight, 2)
    over_y = flip(weight, 4)
    onward = jnp.where(me % 2 == 0, over_x, over_y)
    diagonal = lax.ppermute(onward, "seq", [(s, s ^ (4 if s % 2 == 0 else 2)) for s in range(8)])
    pieces = [(0, weight), (2, over_x), (4, over_y), (6, diagonal)]
    pieces += [(mask ^ 1, flip(piece, 1)) for mask, piece in pieces]
    depth = weight.shape[1]
    whole = jnp.zeros((3, count * depth, weight.shape[2]), weight.dtype)
    for mask, piece in pieces:
        whole = lax.dynamic_update_slice(whole, piece, (0, (me ^ mask) * depth, 0))
    return whole


def project(tokens, in_weight):
    count = lax.axis_size("ch")
    if count != 4:
        gathered = lax.all_gather(tokens, "ch", axis=1, tiled=True)
        weights = gather_weights(in_weight)
        blocks = [
            jnp.dot(gathered, weights[j], preferred_element_type=jnp.float32) for j in range(3)
        ]
        return jnp.concatenate(blocks, axis=1)
    me = lax.axis_index("ch")
    depth = tokens.shape[1]

    def shift(value, pairs):
        return lax.ppermute(value, "ch", pairs)

    up_1 = shift(tokens, [(0, 1), (1, 2), (2, 3)])
    down_1 = shift(tokens, [(1, 0), (2, 1), (3, 2)])
    up_2 = shift(up_1, [(1, 2), (2, 3)])
    down_2 = shift(down_1, [(1, 0), (2, 1)])
    up_3 = shift(up_2, [(2, 3)])
    down_3 = shift(down_2, [(1, 0)])
    weights = gather_weights(in_weight)

    def add_rows(value, source):
        portion = lax.dynamic_slice_in_dim(weights, source * depth, depth, 1)
        return jnp.concatenate(
            [jnp.dot(value, portion[j], preferred_element_type=jnp.float32) for j in range(3)],
            axis=1,
        )

    total = add_rows(tokens, me)
    total += add_rows(up_1, (me + 3) % 4) + add_rows(down_1, (me + 1) % 4)
    total += add_rows(up_2 + down_2, (me + 2) % 4)
    total, up_3, down_3 = lax.optimization_barrier((total, up_3, down_3))
    return total + add_rows(up_3 + down_3, 3 - me)


def exchange_kernel(count, own_ref, tail_ref, states_ref, behind_ref, send_sems, recv_sems):
    me = lax.axis_index("seq")

    def other(offset):
        return {"seq": lax.rem(me + offset, count)}

    barrier = pltpu.get_barrier_semaphore()
    for offset in range(1, count):
        pl.semaphore_signal(
            barrier, inc=1, device_id=other(offset), device_id_type=pl.DeviceIdType.MESH
        )
    pl.semaphore_wait(barrier, count - 1)

    def copy(source, target, slot, offset):
        return pltpu.make_async_remote_copy(
            src_ref=source,
            dst_ref=target,
            send_sem=send_sems.at[slot],
            recv_sem=recv_sems.at[slot],
            device_id=other(offset),
            device_id_type=pl.DeviceIdType.MESH,
        )

    copies = [copy(tail_ref, behind_ref, 0, 1)]
    copies += [copy(own_ref, states_ref.at[me], k, k) for k in range(1, count)]
    for each in copies:
        each.start()
    states_ref[me] = own_ref[...]
    for each in copies:
        each.wait()


def exchange(own, tail):
    count = lax.axis_size("seq")
    return pl.pallas_call(
        lambda *refs: exchange_kernel(count, *refs),
        out_shape=(
            jax.ShapeDtypeStruct((count,) + own.shape, own.dtype),
            jax.ShapeDtypeStruct(tail.shape, tail.dtype),
        ),
        in_specs=[pl.BlockSpec(memory_space=pltpu.VMEM)] * 2,
        out_specs=[pl.BlockSpec(memory_space=pltpu.VMEM)] * 2,
        scratch_shapes=[pltpu.SemaphoreType.DMA((count,)), pltpu.SemaphoreType.DMA((count,))],
        compiler_params=pltpu.CompilerParams(collective_id=0, has_side_effects=True),
    )(own, tail)


def phase_angle(steps, mode_count):
    period = 4 * mode_count
    odd_numbers = 2 * jnp.arange(mode_count) + 1
    turns = steps[:, None] % period * odd_numbers[None, :] % period
    return turns.astype(jnp.float32) * (math.pi / (2 * mode_count))


def damped(decay_rate, steps):
    angle = phase_angle(steps, decay_rate.shape[0])
    magnitude = jnp.exp(-decay_rate[None] * steps.astype(jnp.float32)[:, None, None])
    return (magnitude * jnp.cos(angle)[:, :, None], magnitude * jnp.sin(angle)[:, :, None])


def fourier(rows, initial, count):
    turns = np.outer(2 * np.arange(rows) + 1, np.arange(initial, initial + count)) % (4 * rows)
    angle = turns * (math.pi / (2 * rows))
    return np.cos(angle).astype(np.float32), np.sin(angle).astype(np.float32)


def times(matrix, value):
    return jnp.dot(
        jnp.asarray(matrix), value, precision=lax.Precision.HIGH, preferred_element_type=jnp.float32
    )


def on_device(tokens, in_weight, short_filter, long_taps, decay_rate, residue):
    place = lax.axis_index("seq")
    count = lax.axis_size("seq")
    rows = tokens.shape[0]
    width = in_weight.shape[2]
    modes = decay_rate.shape[0]
    half = 2 * modes
    laps = rows // half

    features = project(tokens, in_weight).astype(jnp.bfloat16)

    coef = residue * jnp.sqrt(-jnp.expm1(-2.0 * decay_rate))
    near_cos, near_sin = damped(decay_rate, jnp.arange(half + 1))
    sign = jnp.where(jnp.arange(laps) % 2 == 0, 1.0, -1.0)[:, None, None]
    far = sign * jnp.exp(
        -decay_rate[None] * (half * jnp.arange(laps)).astype(jnp.float32)[:, None, None]
    )
    near_kernel = jnp.sum(near_cos[:half, None] * far[None] * coef[None, None], axis=2)
    modal_kernel = near_kernel.transpose(1, 0, 2).reshape(rows, width)
    kernel = modal_kernel.at[:TAPS].add(long_taps)
    cos, sin = fourier(rows, 0, rows)
    cos_sin = np.concatenate([cos, -sin], axis=0)
    spectrum = times(cos_sin, kernel) * (1.0 / rows)
    taps_spectrum = times(cos_sin[:, :TAPS], long_taps) * (1.0 / rows)
    kernel_re, kernel_im = spectrum[:rows], spectrum[rows:]
    taps_re, taps_im = taps_spectrum[:rows], taps_spectrum[rows:]
    behind = place - 1 - jnp.arange(count)
    since_re, since_im = damped(decay_rate, jnp.maximum(behind, 0) * rows)
    before = (behind >= 0)[:, None, None]
    since_re = jnp.where(before, since_re, 0.0)
    since_im = jnp.where(before, since_im, 0.0)
    ahead_re = (coef[None] * near_cos[1:]).transpose(1, 0, 2)
    ahead_im = (coef[None] * near_sin[1:]).transpose(1, 0, 2)
    back_re, back_im, back_far = near_cos[:half][::-1], near_sin[:half][::-1], far[::-1]

    head = from_behind(features[rows - (SHORT - 1) :], "seq")
    extended = jnp.concatenate([head, features], axis=0).astype(jnp.float32)
    short_taps = short_filter.reshape(SHORT, 3 * width)
    filtered = sum(
        short_taps[i][None] * extended[SHORT - 1 - i : SHORT - 1 - i + rows] for i in range(SHORT)
    )
    product = (filtered[:, width : 2 * width] * filtered[:, 2 * width :]).astype(jnp.bfloat16)

    product_f = product.astype(jnp.float32)
    by_lap = product_f.reshape(laps, half, width)
    folded = jnp.sum(back_far[:, None] * by_lap[:, :, None, :], axis=0)
    own = jnp.concatenate(
        [jnp.sum(back_re * folded, axis=0), jnp.sum(back_im * folded, axis=0)], axis=0
    ).astype(jnp.bfloat16)
    states, tail = exchange(own, product[rows - TAPS :])
    states = states.astype(jnp.float32)
    tail = jnp.where(place > 0, tail.astype(jnp.float32), 0.0)

    seen = times(cos_sin, product_f)
    seen_re, seen_im = seen[:rows], seen[rows:]
    tail_cos, tail_sin = fourier(rows, -TAPS, TAPS)
    halo = times(np.concatenate([tail_cos, -tail_sin], axis=0), tail)
    halo_re, halo_im = halo[:rows], halo[rows:]
    out_re = kernel_re * seen_re - kernel_im * seen_im + taps_re * halo_re - taps_im * halo_im
    out_im = kernel_re * seen_im + kernel_im * seen_re + taps_re * halo_im + taps_im * halo_re
    local = times(
        np.concatenate([cos.T, -sin.T], axis=1), jnp.concatenate([out_re, out_im], axis=0)
    )

    state_re, state_im = states[:, :modes], states[:, modes:]
    inflow_re = jnp.sum(since_re * state_re - since_im * state_im, axis=0)
    inflow_im = jnp.sum(since_re * state_im + since_im * state_re, axis=0)
    ahead = ahead_re * inflow_re[:, None] - ahead_im * inflow_im[:, None]
    inflow = jnp.sum(far[:, :, None, :] * ahead[None], axis=1).reshape(rows, width)
    return (filtered[:, :width] * (local + inflow)).astype(jnp.bfloat16)


def solution(mesh):
    placed = (
        P("seq", "ch"),
        P(None, "seq", "ch"),
        P(None, None, "ch"),
        P(None, "ch"),
        P(None, "ch"),
        P(None, "ch"),
    )
    return jax.shard_map(
        on_device, mesh=mesh, in_specs=placed, out_specs=P("seq", "ch"), check_vma=False
    )
```

```python
import math

import jax
import jax.numpy as jnp
import numpy as np
from jax import lax
from jax.experimental import pallas as pl
from jax.experimental.pallas import tpu as pltpu
from jax.sharding import PartitionSpec as P

TAPS = 128
SHORT = 7


def from_behind(value, axis):
    count = lax.axis_size(axis)
    return lax.ppermute(value, axis, [(source, source + 1) for source in range(count - 1)])


def flip(value, mask):
    count = lax.axis_size("seq")
    return lax.ppermute(value, "seq", [(s, s ^ mask) for s in range(count)])


def gather_weights(weight, ahead=()):
    count = lax.axis_size("seq")
    if count != 8:
        return lax.all_gather(weight, "seq", axis=1, tiled=True)
    me = lax.axis_index("seq")
    over_x = flip(weight, 2)
    over_y = flip(weight, 4)
    over_x, over_y, *_ = lax.optimization_barrier((over_x, over_y, *ahead))
    by_y = lax.ppermute(over_x, "seq", [(s, s ^ 4) for s in range(0, 8, 2)])
    by_x = lax.ppermute(over_y, "seq", [(s, s ^ 2) for s in range(1, 8, 2)])
    diagonal = jnp.where(me % 2 == 0, by_y, by_x)
    pieces = [(0, weight), (2, over_x), (4, over_y), (6, diagonal)]
    pieces += [(mask ^ 1, flip(piece, 1)) for mask, piece in pieces]
    depth = weight.shape[1]
    whole = jnp.zeros((3, count * depth, weight.shape[2]), weight.dtype)
    for mask, piece in pieces:
        whole = lax.dynamic_update_slice(whole, piece, (0, (me ^ mask) * depth, 0))
    return whole


def project(tokens, in_weight):
    count = lax.axis_size("ch")
    if count != 4:
        gathered = lax.all_gather(tokens, "ch", axis=1, tiled=True)
        weights = gather_weights(in_weight)
        blocks = [
            jnp.dot(gathered, weights[j], preferred_element_type=jnp.float32) for j in range(3)
        ]
        return jnp.concatenate(blocks, axis=1)
    me = lax.axis_index("ch")
    depth = tokens.shape[1]

    def shift(value, pairs):
        return lax.ppermute(value, "ch", pairs)

    up_1 = shift(tokens, [(0, 1), (1, 2), (2, 3)])
    down_1 = shift(tokens, [(1, 0), (2, 1), (3, 2)])
    up_2 = shift(up_1, [(1, 2), (2, 3)])
    down_2 = shift(down_1, [(1, 0), (2, 1)])
    up_3 = shift(up_2, [(2, 3)])
    down_3 = shift(down_2, [(1, 0)])
    weights = gather_weights(in_weight, (up_1, down_1))

    def add_rows(value, source):
        portion = lax.dynamic_slice_in_dim(weights, source * depth, depth, 1)
        return jnp.concatenate(
            [jnp.dot(value, portion[j], preferred_element_type=jnp.float32) for j in range(3)],
            axis=1,
        )

    total = add_rows(tokens, me)
    total += add_rows(up_1, (me + 3) % 4) + add_rows(down_1, (me + 1) % 4)
    total += add_rows(up_2 + down_2, (me + 2) % 4)
    total, up_3, down_3 = lax.optimization_barrier((total, up_3, down_3))
    return total + add_rows(up_3 + down_3, 3 - me)


def exchange_kernel(count, own_ref, tail_ref, states_ref, behind_ref, send_sems, recv_sems):
    me = lax.axis_index("seq")

    def other(offset):
        return {"seq": lax.rem(me + offset, count)}

    barrier = pltpu.get_barrier_semaphore()
    for offset in range(1, count):
        pl.semaphore_signal(
            barrier, inc=1, device_id=other(offset), device_id_type=pl.DeviceIdType.MESH
        )
    pl.semaphore_wait(barrier, count - 1)

    def copy(source, target, slot, offset):
        return pltpu.make_async_remote_copy(
            src_ref=source,
            dst_ref=target,
            send_sem=send_sems.at[slot],
            recv_sem=recv_sems.at[slot],
            device_id=other(offset),
            device_id_type=pl.DeviceIdType.MESH,
        )

    copies = [copy(tail_ref, behind_ref, 0, 1)]
    copies += [copy(own_ref, states_ref.at[me], k, k) for k in range(1, count)]
    for each in copies:
        each.start()
    states_ref[me] = own_ref[...]
    for each in copies:
        each.wait()


def exchange(own, tail):
    count = lax.axis_size("seq")
    return pl.pallas_call(
        lambda *refs: exchange_kernel(count, *refs),
        out_shape=(
            jax.ShapeDtypeStruct((count,) + own.shape, own.dtype),
            jax.ShapeDtypeStruct(tail.shape, tail.dtype),
        ),
        in_specs=[pl.BlockSpec(memory_space=pltpu.VMEM)] * 2,
        out_specs=[pl.BlockSpec(memory_space=pltpu.VMEM)] * 2,
        scratch_shapes=[pltpu.SemaphoreType.DMA((count,)), pltpu.SemaphoreType.DMA((count,))],
        compiler_params=pltpu.CompilerParams(collective_id=0, has_side_effects=True),
    )(own, tail)


def phase_angle(steps, mode_count):
    period = 4 * mode_count
    odd_numbers = 2 * jnp.arange(mode_count) + 1
    turns = steps[:, None] % period * odd_numbers[None, :] % period
    return turns.astype(jnp.float32) * (math.pi / (2 * mode_count))


def damped(decay_rate, steps):
    angle = phase_angle(steps, decay_rate.shape[0])
    magnitude = jnp.exp(-decay_rate[None] * steps.astype(jnp.float32)[:, None, None])
    return (magnitude * jnp.cos(angle)[:, :, None], magnitude * jnp.sin(angle)[:, :, None])


def fourier(rows, initial, count):
    turns = np.outer(2 * np.arange(rows) + 1, np.arange(initial, initial + count)) % (4 * rows)
    angle = turns * (math.pi / (2 * rows))
    return np.cos(angle).astype(np.float32), np.sin(angle).astype(np.float32)


def times(matrix, value):
    return jnp.dot(
        jnp.asarray(matrix), value, precision=lax.Precision.HIGH, preferred_element_type=jnp.float32
    )


def on_device(tokens, in_weight, short_filter, long_taps, decay_rate, residue):
    place = lax.axis_index("seq")
    count = lax.axis_size("seq")
    rows = tokens.shape[0]
    width = in_weight.shape[2]
    modes = decay_rate.shape[0]
    half = 2 * modes
    laps = rows // half

    features = project(tokens, in_weight).astype(jnp.bfloat16)

    coef = residue * jnp.sqrt(-jnp.expm1(-2.0 * decay_rate))
    near_cos, near_sin = damped(decay_rate, jnp.arange(half + 1))
    sign = jnp.where(jnp.arange(laps) % 2 == 0, 1.0, -1.0)[:, None, None]
    far = sign * jnp.exp(
        -decay_rate[None] * (half * jnp.arange(laps)).astype(jnp.float32)[:, None, None]
    )
    near_kernel = jnp.sum(near_cos[:half, None] * far[None] * coef[None, None], axis=2)
    modal_kernel = near_kernel.transpose(1, 0, 2).reshape(rows, width)
    kernel = modal_kernel.at[:TAPS].add(long_taps)
    cos, sin = fourier(rows, 0, rows)
    cos_sin = np.concatenate([cos, -sin], axis=0)
    spectrum = times(cos_sin, kernel) * (1.0 / rows)
    taps_spectrum = times(cos_sin[:, :TAPS], long_taps) * (1.0 / rows)
    kernel_re, kernel_im = spectrum[:rows], spectrum[rows:]
    taps_re, taps_im = taps_spectrum[:rows], taps_spectrum[rows:]
    behind = place - 1 - jnp.arange(count)
    since_re, since_im = damped(decay_rate, jnp.maximum(behind, 0) * rows)
    before = (behind >= 0)[:, None, None]
    since_re = jnp.where(before, since_re, 0.0)
    since_im = jnp.where(before, since_im, 0.0)
    ahead_re = (coef[None] * near_cos[1:]).transpose(1, 0, 2)
    ahead_im = (coef[None] * near_sin[1:]).transpose(1, 0, 2)
    back_re, back_im, back_far = near_cos[:half][::-1], near_sin[:half][::-1], far[::-1]

    head = from_behind(features[rows - (SHORT - 1) :], "seq")
    extended = jnp.concatenate([head, features], axis=0).astype(jnp.float32)
    short_taps = short_filter.reshape(SHORT, 3 * width)
    filtered = sum(
        short_taps[i][None] * extended[SHORT - 1 - i : SHORT - 1 - i + rows] for i in range(SHORT)
    )
    product = (filtered[:, width : 2 * width] * filtered[:, 2 * width :]).astype(jnp.bfloat16)

    product_f = product.astype(jnp.float32)
    by_lap = product_f.reshape(laps, half, width)
    folded = jnp.sum(back_far[:, None] * by_lap[:, :, None, :], axis=0)
    own = jnp.concatenate(
        [jnp.sum(back_re * folded, axis=0), jnp.sum(back_im * folded, axis=0)], axis=0
    ).astype(jnp.bfloat16)
    states, tail = exchange(own, product[rows - TAPS :])
    states = states.astype(jnp.float32)
    tail = jnp.where(place > 0, tail.astype(jnp.float32), 0.0)

    seen = times(cos_sin, product_f)
    seen_re, seen_im = seen[:rows], seen[rows:]
    tail_cos, tail_sin = fourier(rows, -TAPS, TAPS)
    halo = times(np.concatenate([tail_cos, -tail_sin], axis=0), tail)
    halo_re, halo_im = halo[:rows], halo[rows:]
    out_re = kernel_re * seen_re - kernel_im * seen_im + taps_re * halo_re - taps_im * halo_im
    out_im = kernel_re * seen_im + kernel_im * seen_re + taps_re * halo_im + taps_im * halo_re
    local = times(
        np.concatenate([cos.T, -sin.T], axis=1), jnp.concatenate([out_re, out_im], axis=0)
    )

    state_re, state_im = states[:, :modes], states[:, modes:]
    inflow_re = jnp.sum(since_re * state_re - since_im * state_im, axis=0)
    inflow_im = jnp.sum(since_re * state_im + since_im * state_re, axis=0)
    ahead = ahead_re * inflow_re[:, None] - ahead_im * inflow_im[:, None]
    inflow = jnp.sum(far[:, :, None, :] * ahead[None], axis=1).reshape(rows, width)
    return (filtered[:, :width] * (local + inflow)).astype(jnp.bfloat16)


def solution(mesh):
    placed = (
        P("seq", "ch"),
        P(None, "seq", "ch"),
        P(None, None, "ch"),
        P(None, "ch"),
        P(None, "ch"),
        P(None, "ch"),
    )
    return jax.shard_map(
        on_device, mesh=mesh, in_specs=placed, out_specs=P("seq", "ch"), check_vma=False
    )
```

```python
import math

import jax
import jax.numpy as jnp
import numpy as np
from jax import lax
from jax.experimental import pallas as pl
from jax.experimental.pallas import tpu as pltpu
from jax.sharding import PartitionSpec as P

TAPS = 128
SHORT = 7


def from_behind(value, axis):
    count = lax.axis_size(axis)
    return lax.ppermute(value, axis, [(source, source + 1) for source in range(count - 1)])


def flip(value, mask):
    count = lax.axis_size("seq")
    return lax.ppermute(value, "seq", [(s, s ^ mask) for s in range(count)])


def gather_weights(weight, ahead=()):
    count = lax.axis_size("seq")
    if count != 8:
        return lax.all_gather(weight, "seq", axis=1, tiled=True)
    me = lax.axis_index("seq")
    over_x = flip(weight, 2)
    over_y = flip(weight, 4)
    over_x, over_y, *_ = lax.optimization_barrier((over_x, over_y, *ahead))
    onward = jnp.where(me % 2 == 0, over_x, over_y)
    diagonal = lax.ppermute(onward, "seq", [(s, s ^ (4 if s % 2 == 0 else 2)) for s in range(8)])
    pieces = [(0, weight), (2, over_x), (4, over_y), (6, diagonal)]
    pieces += [(mask ^ 1, flip(piece, 1)) for mask, piece in pieces]
    depth = weight.shape[1]
    whole = jnp.zeros((3, count * depth, weight.shape[2]), weight.dtype)
    for mask, piece in pieces:
        whole = lax.dynamic_update_slice(whole, piece, (0, (me ^ mask) * depth, 0))
    return whole


def project(tokens, in_weight):
    count = lax.axis_size("ch")
    if count != 4:
        gathered = lax.all_gather(tokens, "ch", axis=1, tiled=True)
        weights = gather_weights(in_weight)
        blocks = [
            jnp.dot(gathered, weights[j], preferred_element_type=jnp.float32) for j in range(3)
        ]
        return jnp.concatenate(blocks, axis=1)
    me = lax.axis_index("ch")
    depth = tokens.shape[1]

    def shift(value, pairs):
        return lax.ppermute(value, "ch", pairs)

    up_1 = shift(tokens, [(0, 1), (1, 2), (2, 3)])
    down_1 = shift(tokens, [(1, 0), (2, 1), (3, 2)])
    up_2 = shift(up_1, [(1, 2), (2, 3)])
    down_2 = shift(down_1, [(1, 0), (2, 1)])
    up_3 = shift(up_2, [(2, 3)])
    down_3 = shift(down_2, [(1, 0)])
    weights = gather_weights(in_weight, (up_1, down_1))

    def add_rows(value, source):
        portion = lax.dynamic_slice_in_dim(weights, source * depth, depth, 1)
        return jnp.concatenate(
            [jnp.dot(value, portion[j], preferred_element_type=jnp.float32) for j in range(3)],
            axis=1,
        )

    total = add_rows(tokens, me)
    total += add_rows(up_1, (me + 3) % 4) + add_rows(down_1, (me + 1) % 4)
    total += add_rows(up_2 + down_2, (me + 2) % 4)
    total, up_3, down_3 = lax.optimization_barrier((total, up_3, down_3))
    return total + add_rows(up_3 + down_3, 3 - me)


def exchange_kernel(count, own_ref, tail_ref, states_ref, behind_ref, send_sems, recv_sems):
    me = lax.axis_index("seq")

    def other(offset):
        return {"seq": lax.rem(me + offset, count)}

    barrier = pltpu.get_barrier_semaphore()
    for offset in range(1, count):
        pl.semaphore_signal(
            barrier, inc=1, device_id=other(offset), device_id_type=pl.DeviceIdType.MESH
        )
    pl.semaphore_wait(barrier, count - 1)

    def copy(source, target, slot, offset):
        return pltpu.make_async_remote_copy(
            src_ref=source,
            dst_ref=target,
            send_sem=send_sems.at[slot],
            recv_sem=recv_sems.at[slot],
            device_id=other(offset),
            device_id_type=pl.DeviceIdType.MESH,
        )

    copies = [copy(tail_ref, behind_ref, 0, 1)]
    copies += [copy(own_ref, states_ref.at[me], k, k) for k in range(1, count)]
    for each in copies:
        each.start()
    states_ref[me] = own_ref[...]
    for each in copies:
        each.wait()


def exchange(own, tail):
    count = lax.axis_size("seq")
    return pl.pallas_call(
        lambda *refs: exchange_kernel(count, *refs),
        out_shape=(
            jax.ShapeDtypeStruct((count,) + own.shape, own.dtype),
            jax.ShapeDtypeStruct(tail.shape, tail.dtype),
        ),
        in_specs=[pl.BlockSpec(memory_space=pltpu.VMEM)] * 2,
        out_specs=[pl.BlockSpec(memory_space=pltpu.VMEM)] * 2,
        scratch_shapes=[pltpu.SemaphoreType.DMA((count,)), pltpu.SemaphoreType.DMA((count,))],
        compiler_params=pltpu.CompilerParams(collective_id=0, has_side_effects=True),
    )(own, tail)


def phase_angle(steps, mode_count):
    period = 4 * mode_count
    odd_numbers = 2 * jnp.arange(mode_count) + 1
    turns = steps[:, None] % period * odd_numbers[None, :] % period
    return turns.astype(jnp.float32) * (math.pi / (2 * mode_count))


def damped(decay_rate, steps):
    angle = phase_angle(steps, decay_rate.shape[0])
    magnitude = jnp.exp(-decay_rate[None] * steps.astype(jnp.float32)[:, None, None])
    return (magnitude * jnp.cos(angle)[:, :, None], magnitude * jnp.sin(angle)[:, :, None])


def fourier(rows, initial, count):
    turns = np.outer(2 * np.arange(rows) + 1, np.arange(initial, initial + count)) % (4 * rows)
    angle = turns * (math.pi / (2 * rows))
    return np.cos(angle).astype(np.float32), np.sin(angle).astype(np.float32)


def times(matrix, value):
    return jnp.dot(
        jnp.asarray(matrix), value, precision=lax.Precision.HIGH, preferred_element_type=jnp.float32
    )


def on_device(tokens, in_weight, short_filter, long_taps, decay_rate, residue):
    place = lax.axis_index("seq")
    count = lax.axis_size("seq")
    rows = tokens.shape[0]
    width = in_weight.shape[2]
    modes = decay_rate.shape[0]
    half = 2 * modes
    laps = rows // half

    features = project(tokens, in_weight).astype(jnp.bfloat16)

    coef = residue * jnp.sqrt(-jnp.expm1(-2.0 * decay_rate))
    near_cos, near_sin = damped(decay_rate, jnp.arange(half + 1))
    sign = jnp.where(jnp.arange(laps) % 2 == 0, 1.0, -1.0)[:, None, None]
    far = sign * jnp.exp(
        -decay_rate[None] * (half * jnp.arange(laps)).astype(jnp.float32)[:, None, None]
    )
    near_kernel = jnp.sum(near_cos[:half, None] * far[None] * coef[None, None], axis=2)
    modal_kernel = near_kernel.transpose(1, 0, 2).reshape(rows, width)
    kernel = modal_kernel.at[:TAPS].add(long_taps)
    cos, sin = fourier(rows, 0, rows)
    cos_sin = np.concatenate([cos, -sin], axis=0)
    spectrum = times(cos_sin, kernel) * (1.0 / rows)
    taps_spectrum = times(cos_sin[:, :TAPS], long_taps) * (1.0 / rows)
    kernel_re, kernel_im = spectrum[:rows], spectrum[rows:]
    taps_re, taps_im = taps_spectrum[:rows], taps_spectrum[rows:]
    behind = place - 1 - jnp.arange(count)
    since_re, since_im = damped(decay_rate, jnp.maximum(behind, 0) * rows)
    before = (behind >= 0)[:, None, None]
    since_re = jnp.where(before, since_re, 0.0)
    since_im = jnp.where(before, since_im, 0.0)
    ahead_re = (coef[None] * near_cos[1:]).transpose(1, 0, 2)
    ahead_im = (coef[None] * near_sin[1:]).transpose(1, 0, 2)
    back_re, back_im, back_far = near_cos[:half][::-1], near_sin[:half][::-1], far[::-1]

    head = from_behind(features[rows - (SHORT - 1) :], "seq")
    extended = jnp.concatenate([head, features], axis=0).astype(jnp.float32)
    short_taps = short_filter.reshape(SHORT, 3 * width)
    filtered = sum(
        short_taps[i][None] * extended[SHORT - 1 - i : SHORT - 1 - i + rows] for i in range(SHORT)
    )
    product = (filtered[:, width : 2 * width] * filtered[:, 2 * width :]).astype(jnp.bfloat16)

    product_f = product.astype(jnp.float32)
    by_lap = product_f.reshape(laps, half, width)
    folded = jnp.sum(back_far[:, None] * by_lap[:, :, None, :], axis=0)
    own = jnp.concatenate(
        [jnp.sum(back_re * folded, axis=0), jnp.sum(back_im * folded, axis=0)], axis=0
    ).astype(jnp.bfloat16)
    states, tail = exchange(own, product[rows - TAPS :])
    states = states.astype(jnp.float32)
    tail = jnp.where(place > 0, tail.astype(jnp.float32), 0.0)

    seen = times(cos_sin, product_f)
    seen_re, seen_im = seen[:rows], seen[rows:]
    tail_cos, tail_sin = fourier(rows, -TAPS, TAPS)
    halo = times(np.concatenate([tail_cos, -tail_sin], axis=0), tail)
    halo_re, halo_im = halo[:rows], halo[rows:]
    out_re = kernel_re * seen_re - kernel_im * seen_im + taps_re * halo_re - taps_im * halo_im
    out_im = kernel_re * seen_im + kernel_im * seen_re + taps_re * halo_im + taps_im * halo_re
    local = times(
        np.concatenate([cos.T, -sin.T], axis=1), jnp.concatenate([out_re, out_im], axis=0)
    )

    state_re, state_im = states[:, :modes], states[:, modes:]
    inflow_re = jnp.sum(since_re * state_re - since_im * state_im, axis=0)
    inflow_im = jnp.sum(since_re * state_im + since_im * state_re, axis=0)
    ahead = ahead_re * inflow_re[:, None] - ahead_im * inflow_im[:, None]
    inflow = jnp.sum(far[:, :, None, :] * ahead[None], axis=1).reshape(rows, width)
    return (filtered[:, :width] * (local + inflow)).astype(jnp.bfloat16)


def solution(mesh):
    placed = (
        P("seq", "ch"),
        P(None, "seq", "ch"),
        P(None, None, "ch"),
        P(None, "ch"),
        P(None, "ch"),
        P(None, "ch"),
    )
    return jax.shard_map(
        on_device, mesh=mesh, in_specs=placed, out_specs=P("seq", "ch"), check_vma=False
    )
```
